32 devices in a mesh: bins: 4 (over y, x), tiles: 8 (over z, core).
Axes of the slice: x: 2, y: 2, z: 4, core: 2. Of those that a mesh axis runs over, the one named last changes fastest.
Arguments:
- spectrum: float32 [1152, 64, 1440], P('bins', 'tiles'), as said below
- sea_mask: int32 [64, 1440], P('tiles'), may hold values 0 or 1
- ice_mask: int32 [64, 1440], P('tiles'), may hold values 0 or 1
- friction: float32 [64, 1440], P('tiles'), may hold values from 0.2 to 1
- wind_dir: float32 [64, 1440], P('tiles'), may hold values from -3.140625 to 3.140625
- ocean_owner: int32 [8, 16], P('tiles'), may hold values from 0 to 3, as said below
Outputs:
- spectrum_next: float32 [1152, 64, 1440], P('bins', 'tiles')
- stokes_drift: float32 [2, 64, 16, 90], P(None, 'tiles', 'bins')
- wave_stress: float32 [2, 64, 16, 90], P(None, 'tiles', 'bins')
The draws below stay inside these ranges and needn't reach their ends.
Inputs may be any that keep to these rules, and one draw needn't show every extreme that they name: The spectrum is positive everywhere. `ocean_owner`: in every row each owner index appears exactly 4 times.
All inputs are finite; a program needn't handle non-finite values. No bound on the sum of `sea_mask` or of `ice_mask` on one device may be relied on, other than what follows from the above.
Results may differ from the reference program's by a relative error of at most 0.0001.
Values sent between devices are 32-bit elements; how exact they have to be, the bound alone decides.
A program may use at most 192 MiB of HBM per device.

```python
import math
import jax
import jax.numpy as jnp
from jax import lax

NDIR = 36
NFREQ = 32
NBINS = 1152
LAT_DEV = 8
NLON = 1440
LON_BLOCKS = 16
BLK = 90
OWN_BLK = 4
NBANDS = 8
NLAT = 64
STEPS = 4


def draw_spectrum(key, part):
    noise = jax.random.uniform(key, (NDIR * NFREQ, NLAT, NLON), jnp.float32, -1.0, 1.0)
    freq_pos = (jnp.arange(NDIR * NFREQ) // NDIR).astype(jnp.float32)
    profile = jnp.power(1.03, NFREQ - 1 - freq_pos)[:, None, None]
    base = jnp.exp(1.2 * noise)
    return (0.05 * base * profile).astype(jnp.float32)


def shuffle_row(row_key):
    base = jnp.arange(LON_BLOCKS) // OWN_BLK
    return jax.random.permutation(row_key, base)


def draw_ocean_owner(key, part):
    row_keys = jax.random.split(key, NBANDS)
    return jax.vmap(shuffle_row)(row_keys).astype(jnp.int32)


def set_ends(array, stream_key, least, top_value):
    spot = [jax.random.randint(jax.random.fold_in(stream_key, axis), (), 0, length) for axis, length in enumerate(array.shape)]
    longest = array.shape.index(max(array.shape))
    next_to = spot[:longest] + [(spot[longest] + 1) % array.shape[longest]] + spot[longest + 1:]
    return array.at[tuple(spot)].set(least).at[tuple(next_to)].set(top_value)


def block_scale(stream_key, extent, cuts, smallest, top_value):
    def one(dim, shards_of):
        steps = jax.random.uniform(jax.random.fold_in(jax.random.fold_in(stream_key, 6), dim), (shards_of,), jnp.float32, smallest / len(cuts), top_value / len(cuts))
        return jnp.repeat(jnp.exp(steps), extent[dim] // shards_of).reshape((-1,) + (1,) * (len(extent) - dim - 1))

    factor_of = one(*cuts[0])
    for cut in cuts[1:]:
        factor_of = factor_of * one(*cut)
    return factor_of


def setup_inputs(seed: int = 0) -> dict:
    key_list = jax.random.split(jax.random.key(seed), 7)
    return {
        "spectrum": draw_spectrum(jax.random.fold_in(key_list[6], 71), 0),
        "sea_mask": set_ends((jax.random.randint(key_list[1], (NLAT, NLON), 0, 10) < 7).astype(jnp.int32), jax.random.fold_in(key_list[1], 1), 0, 1),
        "ice_mask": set_ends((jax.random.randint(key_list[2], (NLAT, NLON), 0, 6) < 1).astype(jnp.int32), jax.random.fold_in(key_list[2], 1), 0, 1),
        "friction": jnp.clip(jnp.exp(math.log(1.0) - 1.609438 * jax.random.uniform(key_list[3], (NLAT, NLON), jnp.float32) ** block_scale(key_list[3], (NLAT, NLON), ((0, 8),), -0.2, 0.2)), 0.2, 1.0),
        "wind_dir": jnp.clip(jax.random.uniform(key_list[4], (NLAT, NLON), jnp.float32, -3.140625, 3.140625), -3.140625, 3.140625),
        "ocean_owner": draw_ocean_owner(jax.random.fold_in(key_list[6], 71), 0),
    }


courant_max = 0.6
grid_step = 0.25 * math.pi / 180.0


def row_metric(first_row, count, lat_total):
    row_pos = (first_row + jnp.arange(count)).astype(jnp.float32)
    latitude = (row_pos - lat_total / 2 + 0.5) * grid_step
    edge_lat = (lat_total / 2 - 0.5) * grid_step
    return jnp.cos(jnp.asarray(edge_lat, jnp.float32)) / jnp.cos(latitude)


def advance(center, south_row, north_row, sea_open, courant_x, courant_y):
    west_cell = jnp.roll(center, 1, axis=2)
    east_cell = jnp.roll(center, -1, axis=2)
    result = center - jnp.maximum(courant_x, 0.0) * (center - west_cell)
    result = result - jnp.maximum(-courant_x, 0.0) * (center - east_cell)
    result = result - jnp.maximum(courant_y, 0.0) * (center - south_row)
    result = result - jnp.maximum(-courant_y, 0.0) * (center - north_row)
    return result * sea_open


def reference(spectrum, sea_mask, ice_mask, friction, wind_dir, ocean_owner):
    sea_open = sea_mask.astype(jnp.float32)
    ice_cover = ice_mask.astype(jnp.float32)
    metric = row_metric(0, NLAT, NLAT)
    angles = (jnp.arange(NDIR).astype(jnp.float32) + 0.5) * (2.0 * math.pi / NDIR)
    cos_dir = jnp.cos(angles)[:, None, None]
    sin_dir = jnp.sin(angles)[:, None, None]
    alignment = jnp.maximum(jnp.cos(angles[:, None, None] - wind_dir[None]), 0.0)
    blocks = spectrum.reshape(NFREQ, NDIR, NLAT, NLON)

    def advance_freq(totals, scan_item):
        freq_index, spectral = scan_item
        freq_pos = freq_index.astype(jnp.float32)
        speed_ratio = jnp.power(1.1, -freq_pos)
        freq_weight = jnp.power(1.03, freq_pos - (NFREQ - 1))
        courant_x = courant_max * speed_ratio * cos_dir * metric[None, :, None]
        courant_y = courant_max * speed_ratio * sin_dir
        spectral = spectral * sea_open
        for sub_step in range(STEPS):
            padded = jnp.pad(spectral, ((0, 0), (1, 1), (0, 0)))
            spectral = advance(spectral, padded[:, :-2], padded[:, 2:], sea_open, courant_x, courant_y)
        growth = 0.5 * friction[None] ** 2 * freq_weight * alignment
        source = growth * spectral
        updated = (spectral + source) * (1.0 - 0.5 * ice_cover)
        partial_value = jnp.stack([
            jnp.sum(freq_weight * cos_dir * updated, axis=0),
            jnp.sum(freq_weight * sin_dir * updated, axis=0),
            jnp.sum(cos_dir * source, axis=0),
            jnp.sum(sin_dir * source, axis=0)])
        return totals + partial_value, updated

    start = jnp.zeros((4, NLAT, NLON), jnp.float32)
    totals, updated = lax.scan(advance_freq, start, (jnp.arange(NFREQ).astype(jnp.int32), blocks))
    spectrum_next = updated.reshape(NBINS, NLAT, NLON)
    fields = totals.reshape(4, NLAT, LON_BLOCKS, BLK)
    ocean_order = jnp.argsort(ocean_owner, axis=1, stable=True).astype(jnp.int32)
    row_order = jnp.repeat(ocean_order, LAT_DEV, axis=0)
    ocean_fields = jnp.take_along_axis(fields, row_order[None, :, :, None], axis=2)
    return spectrum_next, ocean_fields[:2], ocean_fields[2:]
```

```python
import functools
import math

import jax
import jax.numpy as jnp
import numpy as np
from jax import lax
from jax.experimental import pallas as pl
from jax.experimental.pallas import tpu as pltpu
from jax.sharding import PartitionSpec as P

NDIR = 36
QUAD = NDIR // 4
NFREQ = 32
LON_BLOCKS = 16
STEPS = 4
HALO = 4
LANES = 128
COURANT_MAX = 0.6
GRID_STEP = 0.25 * math.pi / 180.0
MESH = pl.DeviceIdType.MESH
ORDER = (0, 2, 1, 3)


def bin_table():
    freq = np.arange(NFREQ, dtype=np.float64)
    angle = (np.arange(NDIR, dtype=np.float64) + 0.5) * (2.0 * math.pi / NDIR)
    parts = [1.1 ** -freq, 1.03 ** (freq - (NFREQ - 1)), np.cos(angle), np.sin(angle)]
    return np.concatenate(parts).astype(np.float32)


def metric_table(tiles, rows):
    total = tiles * rows
    pos = np.arange(-HALO, total + HALO, dtype=np.float64)
    metric = math.cos((total / 2 - 0.5) * GRID_STEP) / np.cos((pos - total / 2 + 0.5) * GRID_STEP)
    out = np.zeros((tiles, 3, rows, LANES), np.float32)
    for t in range(tiles):
        base = t * rows + HALO
        south = metric[base - HALO:base]
        north = metric[base + rows:base + rows + HALO]
        out[t, 0] = metric[base:base + rows, None]
        out[t, 1] = np.concatenate([south, south])[:, None]
        out[t, 2] = np.concatenate([north, north])[:, None]
    return out


def kernel(dims, tab, owner, metric, sea, ice, friction, wind, spec,
           next_ref, sums_ref,
           field, sea_f, ice_f, fc_f, fs_f, acc, halo_s, snd, rcv, mask_s, mask_r,
           blk, part, gath,
           in_sem, out_sem, snd_sem, rcv_sem, msnd_sem, mrcv_sem, psnd_sem, prcv_sem):
    nk, nb, nt, width, pad = dims
    ntile = pad // LANES
    tail = width - (pad - LANES)
    owned = LON_BLOCKS // nb
    blk_cells = width // LON_BLOCKS
    me = lax.axis_index("bins")
    t = lax.axis_index("tiles")
    has_south = t > 0
    has_north = t < nt - 1

    def in_copy(k, q, h):
        rows = pl.ds((2 * k + h) * NDIR + q * QUAD, QUAD)
        return pltpu.make_async_copy(spec.at[rows], field.at[rows], in_sem.at[k, q, h])

    def out_copy(k, q, h):
        rows = pl.ds((2 * k + h) * NDIR + q * QUAD, QUAD)
        return pltpu.make_async_copy(field.at[rows], next_ref.at[rows], out_sem.at[k, q, h])

    def halo_copy(k, q):
        target = t + 1 if q < 2 else t - 1
        return pltpu.make_async_remote_copy(
            src_ref=snd.at[k, q], dst_ref=rcv.at[k, q],
            send_sem=snd_sem.at[k, q], recv_sem=rcv_sem.at[k, q],
            device_id={"tiles": target}, device_id_type=MESH)

    def mask_copy(side):
        target = t + 1 if side == 0 else t - 1
        return pltpu.make_async_remote_copy(
            src_ref=mask_s.at[side], dst_ref=mask_r.at[side],
            send_sem=msnd_sem.at[side], recv_sem=mrcv_sem.at[side],
            device_id={"tiles": target}, device_id_type=MESH)

    sends = (has_north, has_south)
    takes = (has_south, has_north)

    @pl.loop(0, nk)
    def _(k):
        for q in ORDER:
            for h in range(2):
                in_copy(k, q, h).start()

    barrier = pltpu.get_barrier_semaphore()

    @pl.when(has_south)
    def _():
        pl.semaphore_signal(barrier, inc=1, device_id={"tiles": t - 1}, device_id_type=MESH)

    @pl.when(has_north)
    def _():
        pl.semaphore_signal(barrier, inc=1, device_id={"tiles": t + 1}, device_id_type=MESH)

    for o in range(1, nb):
        pl.semaphore_signal(barrier, inc=1, device_id={"bins": lax.rem(me + o, nb)}, device_id_type=MESH)

    def widen(x):
        return jnp.concatenate([x, jnp.zeros((x.shape[0], pad - width), x.dtype)], axis=1)

    def wide(v):
        return jnp.concatenate([v] * ntile, axis=1)

    row_w = lax.broadcasted_iota(jnp.int32, (8, pad), 0)
    row_1 = lax.broadcasted_iota(jnp.int32, (8, LANES), 0)
    lane_1 = lax.broadcasted_iota(jnp.int32, (8, LANES), 1)

    open_cells = widen(sea[...].astype(jnp.float32))
    sea_f[...] = open_cells
    ice_f[...] = widen(1.0 - 0.5 * ice[...].astype(jnp.float32))
    strength = 0.5 * friction[...] * friction[...]
    fc_f[...] = widen(strength * jnp.cos(wind[...]))
    fs_f[...] = widen(strength * jnp.sin(wind[...]))
    acc[...] = jnp.zeros_like(acc)
    turned = pltpu.roll(open_cells, HALO, 0)
    mask_s[0] = jnp.where(row_w < HALO, turned, open_cells)
    mask_s[1] = jnp.where(row_w < HALO, open_cells, turned)

    for side in range(2):
        @pl.when(jnp.logical_not(takes[side]))
        def _():
            mask_r[side] = jnp.zeros((8, pad), jnp.float32)

            @pl.loop(0, nk)
            def _(k):
                for q in (2 * side, 2 * side + 1):
                    @pl.loop(0, QUAD)
                    def _(i):
                        rcv[k, q, i] = jnp.zeros((8, pad), jnp.float32)

    inner = jnp.logical_and(has_south, has_north)

    @pl.when(inner)
    def _():
        pl.semaphore_wait(barrier, nb + 1)

    @pl.when(jnp.logical_not(inner))
    def _():
        pl.semaphore_wait(barrier, nb)

    for side in range(2):
        @pl.when(sends[side])
        def _():
            mask_copy(side).start()

    @pl.loop(0, nk)
    def _(k):
        for q in ORDER:
            in_copy(k, q, 0).wait()
            in_copy(k, q, 1).wait()

            @pl.when(sends[q // 2])
            def _():
                @pl.loop(0, QUAD)
                def _(i):
                    first = 2 * k * NDIR + q * QUAD + i
                    a = widen(field[first])
                    b = widen(field[first + NDIR])
                    if q < 2:
                        slab = jnp.where(row_w < HALO, pltpu.roll(a, HALO, 0), b)
                        slab = slab * mask_s[0]
                    else:
                        slab = jnp.where(row_w < HALO, a, pltpu.roll(b, HALO, 0))
                        slab = slab * mask_s[1]
                    snd[k, q, i] = slab

                halo_copy(k, q).start()

    for side in range(2):
        @pl.when(takes[side])
        def _():
            mask_copy(side).wait_recv()

    def x_shift(cells, west):
        if west:
            moved = pltpu.roll(cells, 1, 1)
            around = pltpu.roll(cells[:, pad - LANES:], LANES - tail + 1, 1)
            head = jnp.where(lane_1 == 0, around, moved[:, :LANES])
            return jnp.concatenate([head, moved[:, LANES:]], axis=1)
        moved = pltpu.roll(cells, pad - 1, 1)
        around = pltpu.roll(cells[:, :LANES], tail - 1, 1)
        last = jnp.where(lane_1 == tail - 1, around, moved[:, pad - LANES:])
        return jnp.concatenate([moved[:, :pad - LANES], last], axis=1)

    def pair(k, q, i):
        north_going, west = q < 2, q in (0, 3)
        side = 0 if north_going else 1
        turn = 1 if north_going else 7
        d = q * QUAD + i
        first = 2 * k * NDIR + d
        j = me * (2 * nk) + 2 * k
        cos_d, sin_d = tab[2 * NFREQ + d], tab[2 * NFREQ + NDIR + d]
        abs_x = COURANT_MAX * (cos_d if west else -cos_d)
        abs_y = COURANT_MAX * (sin_d if north_going else -sin_d)
        speed = (tab[j], tab[j + 1])
        weight = (tab[NFREQ + j], tab[NFREQ + j + 1])
        ax = (speed[0] * abs_x, speed[1] * abs_x)
        by = (speed[0] * abs_y, speed[1] * abs_y)

        a_h = jnp.where(row_1 < HALO, ax[0], ax[1]) * metric[t, 1 + side]
        b_h = jnp.where(row_1 < HALO, by[0], by[1])
        c_h = wide(1.0 - b_h - a_h)
        a_h, b_h = wide(a_h), wide(b_h)
        cells = rcv[k, q, i]
        for step in range(STEPS - 1):
            upwind = b_h * pltpu.roll(cells, turn, 0) + a_h * x_shift(cells, west)
            cells = c_h * cells + mask_r[side] * upwind
            halo_s[step] = cells

        scaled, gained = None, None
        for h in range(2):
            at = HALO * h + (HALO - 1 if north_going else 0)
            am = ax[h] * metric[t, 0]
            keep = wide(1.0 - by[h] - am)
            am = wide(am)
            cells = widen(field[first + h * NDIR]) * sea_f[...]
            for step in range(STEPS):
                if step == 0:
                    edge = rcv[k, q, i, pl.ds(at, 1), :]
                else:
                    edge = halo_s[step - 1, pl.ds(at, 1), :]
                beside = jnp.where(row_w == (7 if north_going else 0), edge, cells)
                upwind = by[h] * pltpu.roll(beside, turn, 0) + am * x_shift(cells, west)
                cells = keep * cells + sea_f[...] * upwind
            growth = jnp.maximum(
                (weight[h] * cos_d) * fc_f[...] + (weight[h] * sin_d) * fs_f[...], 0.0)
            source = growth * cells
            updated = (cells + source) * ice_f[...]
            field[first + h * NDIR] = updated[:, :width]
            if h == 0:
                scaled, gained = weight[h] * updated, source
            else:
                scaled, gained = scaled + weight[h] * updated, gained + source
        acc[0] += cos_d * scaled
        acc[1] += sin_d * scaled
        acc[2] += cos_d * gained
        acc[3] += sin_d * gained

    @pl.loop(0, nk)
    def _(k):
        for q in ORDER:
            @pl.when(takes[q // 2])
            def _():
                halo_copy(k, q).wait_recv()

            @pl.loop(0, QUAD)
            def _(i):
                pair(k, q, i)

            out_copy(k, q, 0).start()
            out_copy(k, q, 1).start()

    for b in range(LON_BLOCKS):
        tile, off = divmod(b * blk_cells, LANES)
        for f in range(4):
            piece = acc[f, :, tile * LANES:(tile + 1) * LANES]
            if off:
                piece = pltpu.roll(piece, LANES - off, 1)
                if off + blk_cells > LANES:
                    more = acc[f, :, (tile + 1) * LANES:(tile + 2) * LANES]
                    piece = jnp.where(lane_1 < LANES - off, piece, pltpu.roll(more, LANES - off, 1))
            blk[b, f] = piece

    rank = []
    for b in range(LON_BLOCKS):
        mine = owner[0, b]
        before = jnp.int32(0)
        for c in range(LON_BLOCKS):
            if c < b:
                before += (owner[0, c] <= mine).astype(jnp.int32)
            elif c > b:
                before += (owner[0, c] < mine).astype(jnp.int32)
        rank.append(before)

    @pl.loop(0, nb)
    def _(g):
        @pl.loop(0, owned)
        def _(s):
            slot = g * owned + s
            total = jnp.zeros((4, 8, LANES), jnp.float32)
            for b in range(LON_BLOCKS):
                total += jnp.where(rank[b] == slot, 1.0, 0.0) * blk[b]
            part[g, s] = total

    def part_copy(o):
        peer = lax.rem(me + o, nb)
        return pltpu.make_async_remote_copy(
            src_ref=part.at[peer], dst_ref=gath.at[o - 1],
            send_sem=psnd_sem.at[o - 1], recv_sem=prcv_sem.at[o - 1],
            device_id={"bins": peer}, device_id_type=MESH)

    for o in range(1, nb):
        part_copy(o).start()
    for o in range(1, nb):
        part_copy(o).wait_recv()
    for s in range(owned):
        total = part[me, s]
        for o in range(1, nb):
            total += gath[o - 1, s]
        for f in range(4):
            sums_ref[f, s] = total[f, :, :blk_cells]

    for o in range(1, nb):
        part_copy(o).wait_send()
    for side in range(2):
        @pl.when(sends[side])
        def _():
            mask_copy(side).wait_send()

    @pl.loop(0, nk)
    def _(k):
        for q in ORDER:
            @pl.when(sends[q // 2])
            def _():
                halo_copy(k, q).wait_send()

            out_copy(k, q, 0).wait()
            out_copy(k, q, 1).wait()


def shards(nb, nt, spectrum, sea_mask, ice_mask, friction, wind_dir, ocean_owner):
    local_bins, rows, width = spectrum.shape
    nk = local_bins // NDIR // 2
    pad = -(-width // LANES) * LANES
    owned = LON_BLOCKS // nb
    blk_cells = width // LON_BLOCKS
    vmem = pl.BlockSpec(memory_space=pltpu.VMEM)
    smem = pl.BlockSpec(memory_space=pltpu.SMEM)
    hbm = pl.BlockSpec(memory_space=pl.ANY)
    updated, sums = pl.pallas_call(
        functools.partial(kernel, (nk, nb, nt, width, pad)),
        out_shape=(
            jax.ShapeDtypeStruct(spectrum.shape, jnp.float32),
            jax.ShapeDtypeStruct((4, owned, rows, blk_cells), jnp.float32),
        ),
        in_specs=[smem, smem, vmem, vmem, vmem, vmem, vmem, hbm],
        out_specs=(hbm, vmem),
        scratch_shapes=[
            pltpu.VMEM((local_bins, rows, width), jnp.float32),
            pltpu.VMEM((rows, pad), jnp.float32),
            pltpu.VMEM((rows, pad), jnp.float32),
            pltpu.VMEM((rows, pad), jnp.float32),
            pltpu.VMEM((rows, pad), jnp.float32),
            pltpu.VMEM((4, rows, pad), jnp.float32),
            pltpu.VMEM((STEPS - 1, rows, pad), jnp.float32),
            pltpu.VMEM((nk, 4, QUAD, rows, pad), jnp.float32),
            pltpu.VMEM((nk, 4, QUAD, rows, pad), jnp.float32),
            pltpu.VMEM((2, rows, pad), jnp.float32),
            pltpu.VMEM((2, rows, pad), jnp.float32),
            pltpu.VMEM((LON_BLOCKS, 4, rows, LANES), jnp.float32),
            pltpu.VMEM((nb, owned, 4, rows, LANES), jnp.float32),
            pltpu.VMEM((nb - 1, owned, 4, rows, LANES), jnp.float32),
            pltpu.SemaphoreType.DMA((nk, 4, 2)),
            pltpu.SemaphoreType.DMA((nk, 4, 2)),
            pltpu.SemaphoreType.DMA((nk, 4)),
            pltpu.SemaphoreType.DMA((nk, 4)),
            pltpu.SemaphoreType.DMA((2,)),
            pltpu.SemaphoreType.DMA((2,)),
            pltpu.SemaphoreType.DMA((nb - 1,)),
            pltpu.SemaphoreType.DMA((nb - 1,)),
        ],
        compiler_params=pltpu.CompilerParams(
            collective_id=0, has_side_effects=True, vmem_limit_bytes=44 * 1024 * 1024),
        cost_estimate=pl.CostEstimate(
            flops=60 * spectrum.size, bytes_accessed=8 * spectrum.size, transcendentals=0),
        name="wave_step",
    )(bin_table(), ocean_owner, metric_table(nt, rows), sea_mask, ice_mask, friction, wind_dir, spectrum)
    fields = jnp.transpose(sums, (0, 2, 1, 3))
    return updated, fields[:2], fields[2:]


def solution(mesh):
    placed = (
        P("bins", "tiles", None),
        P("tiles", None),
        P("tiles", None),
        P("tiles", None),
        P("tiles", None),
        P("tiles", None),
    )
    return jax.shard_map(
        functools.partial(shards, mesh.shape["bins"], mesh.shape["tiles"]),
        mesh=mesh,
        in_specs=placed,
        out_specs=(
            P("bins", "tiles", None),
            P(None, "tiles", "bins", None),
            P(None, "tiles", "bins", None),
        ),
        check_vma=False,
    )
```

```python
import functools
import math

import jax
import jax.numpy as jnp
import numpy as np
from jax import lax
from jax.experimental import pallas as pl
from jax.experimental.pallas import tpu as pltpu
from jax.sharding import PartitionSpec as P

NDIR = 36
QUAD = NDIR // 4
NFREQ = 32
LON_BLOCKS = 16
STEPS = 4
HALO = 4
LANES = 128
COURANT_MAX = 0.6
GRID_STEP = 0.25 * math.pi / 180.0
MESH = pl.DeviceIdType.MESH
ORDER = (0, 2, 1, 3)


def bin_table():
    freq = np.arange(NFREQ, dtype=np.float64)
    angle = (np.arange(NDIR, dtype=np.float64) + 0.5) * (2.0 * math.pi / NDIR)
    parts = [1.1 ** -freq, 1.03 ** (freq - (NFREQ - 1)), np.cos(angle), np.sin(angle)]
    return np.concatenate(parts).astype(np.float32)


def metric_table(tiles, rows):
    total = tiles * rows
    pos = np.arange(-HALO, total + HALO, dtype=np.float64)
    metric = math.cos((total / 2 - 0.5) * GRID_STEP) / np.cos((pos - total / 2 + 0.5) * GRID_STEP)
    out = np.zeros((tiles, 3, rows, LANES), np.float32)
    for t in range(tiles):
        base = t * rows + HALO
        south = metric[base - HALO:base]
        north = metric[base + rows:base + rows + HALO]
        out[t, 0] = metric[base:base + rows, None]
        out[t, 1] = np.concatenate([south, south])[:, None]
        out[t, 2] = np.concatenate([north, north])[:, None]
    return out


def kernel(dims, tab, owner, metric, sea, ice, friction, wind, spec,
           field, sums_ref,
           sea_f, ice_f, fc_f, fs_f, acc, halo_s, snd, rcv, mask_s, mask_r,
           blk, part, gath,
           in_sem, snd_sem, rcv_sem, msnd_sem, mrcv_sem, psnd_sem, prcv_sem):
    nk, nb, nt, width, pad = dims
    ntile = pad // LANES
    tail = width - (pad - LANES)
    owned = LON_BLOCKS // nb
    blk_cells = width // LON_BLOCKS
    me = lax.axis_index("bins")
    t = lax.axis_index("tiles")
    has_south = t > 0
    has_north = t < nt - 1

    def in_copy(k, q, h):
        rows = pl.ds((2 * k + h) * NDIR + q * QUAD, QUAD)
        return pltpu.make_async_copy(spec.at[rows], field.at[rows], in_sem.at[k, q, h])

    def halo_copy(k, q):
        target = t + 1 if q < 2 else t - 1
        return pltpu.make_async_remote_copy(
            src_ref=snd.at[k, q], dst_ref=rcv.at[k, q],
            send_sem=snd_sem.at[k, q], recv_sem=rcv_sem.at[k, q],
            device_id={"tiles": target}, device_id_type=MESH)

    def mask_copy(side):
        target = t + 1 if side == 0 else t - 1
        return pltpu.make_async_remote_copy(
            src_ref=mask_s.at[side], dst_ref=mask_r.at[side],
            send_sem=msnd_sem.at[side], recv_sem=mrcv_sem.at[side],
            device_id={"tiles": target}, device_id_type=MESH)

    sends = (has_north, has_south)
    takes = (has_south, has_north)

    @pl.loop(0, nk)
    def _(k):
        for q in ORDER:
            for h in range(2):
                in_copy(k, q, h).start()

    barrier = pltpu.get_barrier_semaphore()

    @pl.when(has_south)
    def _():
        pl.semaphore_signal(barrier, inc=1, device_id={"tiles": t - 1}, device_id_type=MESH)

    @pl.when(has_north)
    def _():
        pl.semaphore_signal(barrier, inc=1, device_id={"tiles": t + 1}, device_id_type=MESH)

    for o in range(1, nb):
        pl.semaphore_signal(barrier, inc=1, device_id={"bins": lax.rem(me + o, nb)}, device_id_type=MESH)

    def widen(x):
        return jnp.concatenate([x, jnp.zeros((x.shape[0], pad - width), x.dtype)], axis=1)

    def wide(v):
        return jnp.concatenate([v] * ntile, axis=1)

    row_w = lax.broadcasted_iota(jnp.int32, (8, pad), 0)
    row_1 = lax.broadcasted_iota(jnp.int32, (8, LANES), 0)
    lane_1 = lax.broadcasted_iota(jnp.int32, (8, LANES), 1)

    open_cells = widen(sea[...].astype(jnp.float32))
    sea_f[...] = open_cells
    ice_f[...] = widen(1.0 - 0.5 * ice[...].astype(jnp.float32))
    strength = 0.5 * friction[...] * friction[...]
    fc_f[...] = widen(strength * jnp.cos(wind[...]))
    fs_f[...] = widen(strength * jnp.sin(wind[...]))
    acc[...] = jnp.zeros_like(acc)
    turned = pltpu.roll(open_cells, HALO, 0)
    mask_s[0] = jnp.where(row_w < HALO, turned, open_cells)
    mask_s[1] = jnp.where(row_w < HALO, open_cells, turned)

    for side in range(2):
        @pl.when(jnp.logical_not(takes[side]))
        def _():
            mask_r[side] = jnp.zeros((8, pad), jnp.float32)

            @pl.loop(0, nk)
            def _(k):
                for q in (2 * side, 2 * side + 1):
                    @pl.loop(0, QUAD)
                    def _(i):
                        rcv[k, q, i] = jnp.zeros((8, pad), jnp.float32)

    inner = jnp.logical_and(has_south, has_north)

    @pl.when(inner)
    def _():
        pl.semaphore_wait(barrier, nb + 1)

    @pl.when(jnp.logical_not(inner))
    def _():
        pl.semaphore_wait(barrier, nb)

    for side in range(2):
        @pl.when(sends[side])
        def _():
            mask_copy(side).start()

    @pl.loop(0, nk)
    def _(k):
        for q in ORDER:
            in_copy(k, q, 0).wait()
            in_copy(k, q, 1).wait()

            @pl.when(sends[q // 2])
            def _():
                @pl.loop(0, QUAD)
                def _(i):
                    first = 2 * k * NDIR + q * QUAD + i
                    a = widen(field[first])
                    b = widen(field[first + NDIR])
                    if q < 2:
                        slab = jnp.where(row_w < HALO, pltpu.roll(a, HALO, 0), b)
                        slab = slab * mask_s[0]
                    else:
                        slab = jnp.where(row_w < HALO, a, pltpu.roll(b, HALO, 0))
                        slab = slab * mask_s[1]
                    snd[k, q, i] = slab

                halo_copy(k, q).start()

    for side in range(2):
        @pl.when(takes[side])
        def _():
            mask_copy(side).wait_recv()

    def x_shift(cells, west):
        if west:
            moved = pltpu.roll(cells, 1, 1)
            around = pltpu.roll(cells[:, pad - LANES:], LANES - tail + 1, 1)
            head = jnp.where(lane_1 == 0, around, moved[:, :LANES])
            return jnp.concatenate([head, moved[:, LANES:]], axis=1)
        moved = pltpu.roll(cells, pad - 1, 1)
        around = pltpu.roll(cells[:, :LANES], tail - 1, 1)
        last = jnp.where(lane_1 == tail - 1, around, moved[:, pad - LANES:])
        return jnp.concatenate([moved[:, :pad - LANES], last], axis=1)

    def pair(k, q, i):
        north_going, west = q < 2, q in (0, 3)
        side = 0 if north_going else 1
        turn = 1 if north_going else 7
        d = q * QUAD + i
        first = 2 * k * NDIR + d
        j = me * (2 * nk) + 2 * k
        cos_d, sin_d = tab[2 * NFREQ + d], tab[2 * NFREQ + NDIR + d]
        abs_x = COURANT_MAX * (cos_d if west else -cos_d)
        abs_y = COURANT_MAX * (sin_d if north_going else -sin_d)
        speed = (tab[j], tab[j + 1])
        weight = (tab[NFREQ + j], tab[NFREQ + j + 1])
        ax = (speed[0] * abs_x, speed[1] * abs_x)
        by = (speed[0] * abs_y, speed[1] * abs_y)

        a_h = jnp.where(row_1 < HALO, ax[0], ax[1]) * metric[t, 1 + side]
        b_h = jnp.where(row_1 < HALO, by[0], by[1])
        c_h = wide(1.0 - b_h - a_h)
        a_h, b_h = wide(a_h), wide(b_h)
        cells = rcv[k, q, i]
        for step in range(STEPS - 1):
            upwind = b_h * pltpu.roll(cells, turn, 0) + a_h * x_shift(cells, west)
            cells = c_h * cells + mask_r[side] * upwind
            halo_s[step] = cells

        scaled, gained = None, None
        for h in range(2):
            at = HALO * h + (HALO - 1 if north_going else 0)
            am = ax[h] * metric[t, 0]
            keep = wide(1.0 - by[h] - am)
            am = wide(am)
            cells = widen(field[first + h * NDIR]) * sea_f[...]
            for step in range(STEPS):
                if step == 0:
                    edge = rcv[k, q, i, pl.ds(at, 1), :]
                else:
                    edge = halo_s[step - 1, pl.ds(at, 1), :]
                beside = jnp.where(row_w == (7 if north_going else 0), edge, cells)
                upwind = by[h] * pltpu.roll(beside, turn, 0) + am * x_shift(cells, west)
                cells = keep * cells + sea_f[...] * upwind
            growth = jnp.maximum(
                (weight[h] * cos_d) * fc_f[...] + (weight[h] * sin_d) * fs_f[...], 0.0)
            source = growth * cells
            updated = (cells + source) * ice_f[...]
            field[first + h * NDIR] = updated[:, :width]
            if h == 0:
                scaled, gained = weight[h] * updated, source
            else:
                scaled, gained = scaled + weight[h] * updated, gained + source
        acc[0] += cos_d * scaled
        acc[1] += sin_d * scaled
        acc[2] += cos_d * gained
        acc[3] += sin_d * gained

    @pl.loop(0, nk)
    def _(k):
        for q in ORDER:
            @pl.when(takes[q // 2])
            def _():
                halo_copy(k, q).wait_recv()

            @pl.loop(0, QUAD)
            def _(i):
                pair(k, q, i)


    for b in range(LON_BLOCKS):
        tile, off = divmod(b * blk_cells, LANES)
        for f in range(4):
            piece = acc[f, :, tile * LANES:(tile + 1) * LANES]
            if off:
                piece = pltpu.roll(piece, LANES - off, 1)
                if off + blk_cells > LANES:
                    more = acc[f, :, (tile + 1) * LANES:(tile + 2) * LANES]
                    piece = jnp.where(lane_1 < LANES - off, piece, pltpu.roll(more, LANES - off, 1))
            blk[b, f] = piece

    rank = []
    for b in range(LON_BLOCKS):
        mine = owner[0, b]
        before = jnp.int32(0)
        for c in range(LON_BLOCKS):
            if c < b:
                before += (owner[0, c] <= mine).astype(jnp.int32)
            elif c > b:
                before += (owner[0, c] < mine).astype(jnp.int32)
        rank.append(before)

    @pl.loop(0, nb)
    def _(g):
        @pl.loop(0, owned)
        def _(s):
            slot = g * owned + s
            total = jnp.zeros((4, 8, LANES), jnp.float32)
            for b in range(LON_BLOCKS):
                total += jnp.where(rank[b] == slot, 1.0, 0.0) * blk[b]
            part[g, s] = total

    def part_copy(o):
        peer = lax.rem(me + o, nb)
        return pltpu.make_async_remote_copy(
            src_ref=part.at[peer], dst_ref=gath.at[o - 1],
            send_sem=psnd_sem.at[o - 1], recv_sem=prcv_sem.at[o - 1],
            device_id={"bins": peer}, device_id_type=MESH)

    for o in range(1, nb):
        part_copy(o).start()
    for o in range(1, nb):
        part_copy(o).wait_recv()
    for s in range(owned):
        total = part[me, s]
        for o in range(1, nb):
            total += gath[o - 1, s]
        for f in range(4):
            sums_ref[f, s] = total[f, :, :blk_cells]

    for o in range(1, nb):
        part_copy(o).wait_send()
    for side in range(2):
        @pl.when(sends[side])
        def _():
            mask_copy(side).wait_send()

    @pl.loop(0, nk)
    def _(k):
        for q in ORDER:
            @pl.when(sends[q // 2])
            def _():
                halo_copy(k, q).wait_send()


def shards(nb, nt, spectrum, sea_mask, ice_mask, friction, wind_dir, ocean_owner):
    local_bins, rows, width = spectrum.shape
    nk = local_bins // NDIR // 2
    pad = -(-width // LANES) * LANES
    owned = LON_BLOCKS // nb
    blk_cells = width // LON_BLOCKS
    vmem = pl.BlockSpec(memory_space=pltpu.VMEM)
    smem = pl.BlockSpec(memory_space=pltpu.SMEM)
    hbm = pl.BlockSpec(memory_space=pl.ANY)
    updated, sums = pl.pallas_call(
        functools.partial(kernel, (nk, nb, nt, width, pad)),
        out_shape=(
            jax.ShapeDtypeStruct(spectrum.shape, jnp.float32),
            jax.ShapeDtypeStruct((4, owned, rows, blk_cells), jnp.float32),
        ),
        in_specs=[smem, smem, vmem, vmem, vmem, vmem, vmem, hbm],
        out_specs=(vmem, vmem),
        scratch_shapes=[
            pltpu.VMEM((rows, pad), jnp.float32),
            pltpu.VMEM((rows, pad), jnp.float32),
            pltpu.VMEM((rows, pad), jnp.float32),
            pltpu.VMEM((rows, pad), jnp.float32),
            pltpu.VMEM((4, rows, pad), jnp.float32),
            pltpu.VMEM((STEPS - 1, rows, pad), jnp.float32),
            pltpu.VMEM((nk, 4, QUAD, rows, pad), jnp.float32),
            pltpu.VMEM((nk, 4, QUAD, rows, pad), jnp.float32),
            pltpu.VMEM((2, rows, pad), jnp.float32),
            pltpu.VMEM((2, rows, pad), jnp.float32),
            pltpu.VMEM((LON_BLOCKS, 4, rows, LANES), jnp.float32),
            pltpu.VMEM((nb, owned, 4, rows, LANES), jnp.float32),
            pltpu.VMEM((nb - 1, owned, 4, rows, LANES), jnp.float32),
            pltpu.SemaphoreType.DMA((nk, 4, 2)),
            pltpu.SemaphoreType.DMA((nk, 4)),
            pltpu.SemaphoreType.DMA((nk, 4)),
            pltpu.SemaphoreType.DMA((2,)),
            pltpu.SemaphoreType.DMA((2,)),
            pltpu.SemaphoreType.DMA((nb - 1,)),
            pltpu.SemaphoreType.DMA((nb - 1,)),
        ],
        compiler_params=pltpu.CompilerParams(
            collective_id=0, has_side_effects=True, vmem_limit_bytes=40 * 1024 * 1024),
        cost_estimate=pl.CostEstimate(
            flops=60 * spectrum.size, bytes_accessed=8 * spectrum.size, transcendentals=0),
        name="wave_step",
    )(bin_table(), ocean_owner, metric_table(nt, rows), sea_mask, ice_mask, friction, wind_dir, spectrum)
    fields = jnp.transpose(sums, (0, 2, 1, 3))
    return updated, fields[:2], fields[2:]


def solution(mesh):
    placed = (
        P("bins", "tiles", None),
        P("tiles", None),
        P("tiles", None),
        P("tiles", None),
        P("tiles", None),
        P("tiles", None),
    )
    return jax.shard_map(
        functools.partial(shards, mesh.shape["bins"], mesh.shape["tiles"]),
        mesh=mesh,
        in_specs=placed,
        out_specs=(
            P("bins", "tiles", None),
            P(None, "tiles", "bins", None),
            P(None, "tiles", "bins", None),
        ),
        check_vma=False,
    )
```
